32 devices in a mesh: dp: 16 (over z, x, core), rep: 2 (over y).
Axes of the slice: x: 2, y: 2, z: 4, core: 2. Of those that a mesh axis runs over, the one named last changes fastest.
Arguments:
- hidden_in: bfloat16 [128, 512, 576], P(('dp', 'rep')), may hold values from -6 to 6
- segment_ids: int32 [128, 512], P(('dp', 'rep')), may hold values from 0 to 5, never falling along the last dimension, each value on 1 to 256 neighbouring positions
- gain_attn: bfloat16 [576], replicated, may hold values from 0.099609375 to 1.8984375
- w_query: bfloat16 [331776], P('dp'), may hold values from -0.25 to 0.25
- w_key: bfloat16 [110592], P('dp'), may hold values from -0.25 to 0.25
- w_value: bfloat16 [110592], P('dp'), may hold values from -0.25 to 0.25
- w_out: bfloat16 [331776], P('dp'), may hold values from -1 to 1
- gain_mlp: bfloat16 [576], replicated, may hold values from 0.099609375 to 1.8984375
- w_gate: bfloat16 [884736], P('dp'), may hold values from -0.25 to 0.25
- w_up: bfloat16 [884736], P('dp'), may hold values from -0.25 to 0.25
- w_down: bfloat16 [884736], P('dp'), may hold values from -0.21875 to 0.21875
- cotangent: bfloat16 [128, 512, 576], P(('dp', 'rep')), may hold values from -6 to 6
Outputs:
- hidden_out: bfloat16 [128, 512, 576], P(('dp', 'rep'))
- grad_hidden: bfloat16 [128, 512, 576], P(('dp', 'rep'))
- grad_gain_attn: float32 [576], replicated
- grad_query: float32 [331776], P('dp')
- grad_key: float32 [110592], P('dp')
- grad_value: float32 [110592], P('dp')
- grad_out: float32 [331776], P('dp')
- grad_gain_mlp: float32 [576], replicated
- grad_gate: float32 [884736], P('dp')
- grad_up: float32 [884736], P('dp')
- grad_down: float32 [884736], P('dp')
The draws below stay inside these ranges and needn't reach their ends.
Inputs may be any that keep to these rules, and one draw needn't show every extreme that they name: `segment_ids`: within each sequence the numbers never fall; one document holds at most half of 512 tokens.
All inputs are finite; a program needn't handle non-finite values.
Results may differ from the reference program's by a relative error of at most 0.014.
Values may be sent and summed in bfloat16 or wider, within the bound.
A program may use at most 192 MiB of HBM per device.

```python
import math
import jax
import jax.numpy as jnp
import numpy as np
from jax import lax

D = 576
HEADS = 9
KV_HEADS = 3
HEAD_DIM = 64
FF = 1536
SEQ = 512
DOCS = 6
SEQS = 128
KV_W = 192


def block_scale(key, extent, pieces, low, largest):
    def one(dim, blocks):
        heights = jax.random.uniform(jax.random.fold_in(jax.random.fold_in(key, 6), dim), (blocks,), jnp.float32, low / len(pieces), largest / len(pieces))
        return jnp.repeat(jnp.exp(heights), extent[dim] // blocks).reshape((-1,) + (1,) * (len(extent) - dim - 1))

    factor_of = one(*pieces[0])
    for cut in pieces[1:]:
        factor_of = factor_of * one(*cut)
    return factor_of


def split_up(amount, total, most, lean):
    loads = [(1 << 20) // math.isqrt(rank ** lean) + 1 for rank in range(2, amount + 1)]
    rest, holding = total - most - (amount - 1), [1] * (amount - 1)
    while rest > 0:
        movable = [i for i in range(amount - 1) if holding[i] < most]
        mass, budget = sum([loads[i] for i in movable]), rest
        for i in movable:
            addition = min(most - holding[i], max(1, budget * loads[i] // mass), rest)
            holding[i] = holding[i] + addition
            rest = rest - addition
    return np.array([most] + holding)


def uneven(own_key, amount, total, reach, lean):
    if amount == 2:
        one = jax.random.randint(own_key, (), max(1, total - reach), min(reach, total - 1) + 1)
        return jnp.stack([one, total - one])
    sizes = jnp.asarray(split_up(amount, total, reach, lean), jnp.int32)
    couples = (amount - 1) // 2
    source_of, sink = sizes[1:1 + 2 * couples:2], sizes[2:2 + 2 * couples:2]
    slack = jnp.minimum(source_of - 1, reach - sink)
    shifted = jax.random.randint(jax.random.fold_in(own_key, 1), (couples,), 0, 1 << 20) % (slack + 1)
    sizes = sizes.at[1:1 + 2 * couples:2].set(source_of - shifted).at[2:2 + 2 * couples:2].set(sink + shifted)
    return sizes[jax.random.permutation(jax.random.fold_in(own_key, 2), amount)]


def normal_values(own_key, dims, spread, most, split=(), held_as=jnp.bfloat16):
    values = jax.random.normal(own_key, dims, jnp.float32) * spread
    if len(split) > 0:
        values = block_scale(own_key, dims, split, -0.22, 0.18) * values
    return jnp.clip(values, min=-most, max=most).astype(held_as)


def setup_inputs(seed: int = 0) -> dict:
    splits = jax.random.split(jax.random.key(seed), 13)
    hidden_in = normal_values(splits[0], (SEQS, SEQ, D), 1.0, 6.0, ((0, 32),))
    segment_ids = jax.vmap(lambda own: jnp.searchsorted(jnp.cumsum(uneven(own, DOCS, SEQ, SEQ // 2, 2)), jnp.arange(SEQ), side="right"))(jax.random.split(splits[1], SEQS)).reshape((SEQS, SEQ)).astype(jnp.int32)
    gain_attn = jnp.clip(1.0 + 0.18 * jax.random.normal(splits[2], (D,), jnp.float32), 0.099609375, 1.8984375).astype(jnp.bfloat16)
    w_query = normal_values(splits[3], (D * D,), D ** -0.5, 0.25, ((0, 16),))
    w_key = normal_values(splits[4], (D * KV_W,), D ** -0.5, 0.25, ((0, 16),))
    w_value = normal_values(splits[5], (D * KV_W,), D ** -0.5, 0.25, ((0, 16),))
    w_out = normal_values(splits[6], (D * D,), (D // 16) ** -0.5, 1.0, ((0, 16),))
    gain_mlp = jnp.clip(1.0 + 0.18 * jax.random.normal(splits[7], (D,), jnp.float32), 0.099609375, 1.8984375).astype(jnp.bfloat16)
    w_gate = normal_values(splits[8], (D * FF,), D ** -0.5, 0.25, ((0, 16),))
    w_up = normal_values(splits[9], (D * FF,), D ** -0.5, 0.25, ((0, 16),))
    w_down = normal_values(splits[10], (FF * D,), (FF // 2) ** -0.5, 0.21875, ((0, 16),))
    cotangent = normal_values(splits[11], (SEQS, SEQ, D), 1.0, 6.0, ((0, 32),))
    return dict(hidden_in=hidden_in, segment_ids=segment_ids, gain_attn=gain_attn, w_query=w_query, w_key=w_key, w_value=w_value, w_out=w_out, gain_mlp=gain_mlp, w_gate=w_gate, w_up=w_up, w_down=w_down, cotangent=cotangent)


EPS = 1e-05
THETA = 100000.0
HIGHEST = lax.Precision.HIGHEST

@jax.custom_vjp
def low(v):
    return lax.optimization_barrier(v.astype(jnp.bfloat16)).astype(jnp.float32)

@jax.custom_vjp
def low_back(v):
    return v

def low_keep(v):
    return (low(v), None)

def low_pass(kept, grad):
    return (grad,)

def back_keep(v):
    return (v, None)

def back_low(kept, grad):
    return (low(grad),)
low.defvjp(low_keep, low_pass)
low_back.defvjp(back_keep, back_low)

def place_mask(segments):
    length = segments.shape[0]
    ladder = jnp.arange(length, dtype=jnp.int32)
    same_doc = segments[:, None] == segments[None, :]
    earlier = ladder[None, :] <= ladder[:, None]
    allowed = jnp.logical_and(same_doc, earlier)
    places = lax.optimization_barrier(jnp.sum(allowed.astype(jnp.int32), axis=1)) - 1
    return (places, allowed)

def rotary_tables(places):
    half_dim = HEAD_DIM // 2
    inverse = THETA ** (-(jnp.arange(half_dim, dtype=jnp.float32) * (2.0 / HEAD_DIM)))
    angles = places.astype(jnp.float32)[:, None] * inverse[None, :]
    angles = jnp.concatenate([angles, angles], axis=1)
    return (jnp.cos(angles), jnp.sin(angles))

def rotate(vectors, cosine, sine_table):
    half_dim = vectors.shape[-1] // 2
    turned = jnp.concatenate([-vectors[..., half_dim:], vectors[..., :half_dim]], axis=-1)
    return vectors * cosine[:, None, :] + turned * sine_table[:, None, :]

def rms_norm(row_data, gain_row):
    inv_scale = lax.rsqrt(lax.optimization_barrier(jnp.mean(row_data * row_data, axis=-1, keepdims=True)) + EPS)
    return row_data * inv_scale * gain_row

def attend(queries, keys_rot, values, allowed):
    length = queries.shape[0]
    group_size = HEADS // KV_HEADS
    grouped = queries.reshape(length, KV_HEADS, group_size, HEAD_DIM)
    scores = jnp.einsum('qkgd,skd->kgqs', grouped, keys_rot, precision=HIGHEST) * HEAD_DIM ** (-0.5)
    scores = low_back(scores)
    scores = jnp.where(allowed[None, None], scores, -1e+30)
    row_max = lax.optimization_barrier(jnp.max(scores, axis=-1, keepdims=True))
    raised = jnp.exp(scores - row_max)
    shares = low(raised / lax.optimization_barrier(jnp.sum(raised, axis=-1, keepdims=True)))
    mixed_heads = jnp.einsum('kgqs,skd->qkgd', shares, values, precision=HIGHEST)
    return mixed_heads.reshape(length, HEADS * HEAD_DIM)

def layer(hidden, gain_attn, w_query, w_key, w_value, w_out, gain_mlp, w_gate, w_up, w_down, cosine, sine_table, allowed):
    seq_count, length = (hidden.shape[0], hidden.shape[1])
    row_data = hidden.reshape(seq_count * length, D)
    normed = low(rms_norm(row_data, gain_attn))
    queries = low_back(jnp.dot(normed, w_query, precision=HIGHEST)).reshape(seq_count, length, HEADS, HEAD_DIM)
    keys_raw = low_back(jnp.dot(normed, w_key, precision=HIGHEST)).reshape(seq_count, length, KV_HEADS, HEAD_DIM)
    values = low(low_back(jnp.dot(normed, w_value, precision=HIGHEST))).reshape(seq_count, length, KV_HEADS, HEAD_DIM)
    queries_rot = low(jax.vmap(rotate)(queries, cosine, sine_table))
    keys_rot = low(jax.vmap(rotate)(keys_raw, cosine, sine_table))
    mixed_heads = lax.map(lambda seq_items: jax.checkpoint(attend)(*seq_items), (queries_rot, keys_rot, values, allowed))
    mixed_rows = low(low_back(mixed_heads.reshape(seq_count * length, D)))
    middle = row_data + low_back(jnp.dot(mixed_rows, w_out, precision=HIGHEST))
    normed_mlp = low(rms_norm(middle, gain_mlp))
    gate_out = low_back(jnp.dot(normed_mlp, w_gate, precision=HIGHEST))
    up_out = low_back(jnp.dot(normed_mlp, w_up, precision=HIGHEST))
    hidden_act = low(jax.nn.silu(gate_out) * up_out)
    result = middle + low_back(jnp.dot(hidden_act, w_down, precision=HIGHEST))
    return result.reshape(seq_count, length, D)

def reference(hidden_in, segment_ids, gain_attn, w_query, w_key, w_value, w_out, gain_mlp, w_gate, w_up, w_down, cotangent):
    per_step = 8
    step_count = hidden_in.shape[0] // per_step
    kv_width = KV_HEADS * HEAD_DIM
    params = (gain_attn.astype(jnp.float32), w_query.astype(jnp.float32).reshape(D, D), w_key.astype(jnp.float32).reshape(D, kv_width), w_value.astype(jnp.float32).reshape(D, kv_width), w_out.astype(jnp.float32).reshape(D, D), gain_mlp.astype(jnp.float32), w_gate.astype(jnp.float32).reshape(D, FF), w_up.astype(jnp.float32).reshape(D, FF), w_down.astype(jnp.float32).reshape(FF, D))

    def advance(totals, step_items):
        hidden_part, segment_part, cotangent_part = step_items
        places, allowed = jax.vmap(place_mask)(segment_part)
        cosine, sine_table = jax.vmap(rotary_tables)(places)

        def forward_only(hidden, *weights):
            return layer(hidden, *weights, cosine, sine_table, allowed)
        result, pull_back = jax.vjp(forward_only, hidden_part.astype(jnp.float32), *params)
        gradients = pull_back(cotangent_part.astype(jnp.float32))
        totals = tuple((running + new_grad for running, new_grad in zip(totals, gradients[1:])))
        return (totals, (result.astype(jnp.bfloat16), gradients[0].astype(jnp.bfloat16)))
    zeros_init = tuple((jnp.zeros_like(weight_arr) for weight_arr in params))
    stacked = (hidden_in.reshape(step_count, per_step, SEQ, D), segment_ids.reshape(step_count, per_step, SEQ), cotangent.reshape(step_count, per_step, SEQ, D))
    totals, (outputs, input_grads) = lax.scan(advance, zeros_init, stacked)
    return (outputs.reshape(hidden_in.shape), input_grads.reshape(hidden_in.shape), totals[0], totals[1].reshape(-1), totals[2].reshape(-1), totals[3].reshape(-1), totals[4].reshape(-1), totals[5], totals[6].reshape(-1), totals[7].reshape(-1), totals[8].reshape(-1))
```

```python
import functools

import jax
import jax.numpy as jnp
from jax import lax
from jax.experimental import pallas as pl
from jax.experimental.pallas import tpu as pltpu
from jax.sharding import PartitionSpec as P

D = 576
HEADS = 9
KV_HEADS = 3
GROUP = HEADS // KV_HEADS
HEAD_DIM = 64
HALF = HEAD_DIM // 2
KV_W = KV_HEADS * HEAD_DIM
QKV = D + 2 * KV_W
FF = 1536
SEQ = 512
QB = 256

EPS = 1e-05
THETA = 100000.0
SCALE = HEAD_DIM ** (-0.5)
F32 = jnp.float32
BF16 = jnp.bfloat16

BLOCKS = ((0, QB, 0), (QB, SEQ, QB))
ROWS = QB + SEQ


def dot(a, b, ca, cb):
    return lax.dot_general(a, b, (((ca,), (cb,)), ((), ())), preferred_element_type=F32)


def turn_t(u):
    return jnp.concatenate([-u[HALF:], u[:HALF]], axis=0)


def attend_kernel(qkv_ref, cos_ref, sin_ref, start_ref, p_ref, o_ref, q_ref, k_ref, v_ref, bias_ref):
    cos, sin = cos_ref[...], sin_ref[...]
    start = start_ref[0]
    key_at = lax.broadcasted_iota(jnp.int32, (SEQ, SEQ), 0)
    query_at = lax.broadcasted_iota(jnp.int32, (SEQ, SEQ), 1)
    ok = jnp.logical_and(key_at <= query_at, key_at >= start)
    bias_ref[...] = jnp.where(ok, 0.0, -1e30)
    v_ref[...] = qkv_ref[D + KV_W :, :].astype(BF16)
    for g in range(KV_HEADS):
        raw = qkv_ref[D + g * HEAD_DIM : D + (g + 1) * HEAD_DIM, :]
        kt = raw * cos + turn_t(raw) * sin
        k_ref[g * HEAD_DIM : (g + 1) * HEAD_DIM, :] = kt.astype(BF16)
        k = kt.T.astype(BF16)
        vt = v_ref[g * HEAD_DIM : (g + 1) * HEAD_DIM, :]
        for j in range(GROUP):
            h = g * GROUP + j
            rows = slice(h * HEAD_DIM, (h + 1) * HEAD_DIM)
            raw = qkv_ref[rows, :]
            qt = (raw * cos + turn_t(raw) * sin).astype(BF16) * jnp.asarray(SCALE, BF16)
            q_ref[rows, :] = qt
            for q0, nk, r0 in BLOCKS:
                st = dot(k[:nk], qt[:, q0 : q0 + QB], 1, 0) + bias_ref[:nk, q0 : q0 + QB]
                top = jnp.max(st, axis=0, keepdims=True)
                e = jnp.exp(st - top)
                total = jnp.sum(e, axis=0, keepdims=True)
                share = (e * (1.0 / total)).astype(BF16)
                p_ref[0, h, r0 : r0 + nk, :] = share
                o_ref[rows, q0 : q0 + QB] = dot(vt[:, :nk], share, 1, 0).astype(BF16)


def attend_forward(qkv, cos, sin, start):
    tokens = qkv.shape[1]
    seqs = tokens // SEQ
    col = lambda rows: pl.BlockSpec((rows, SEQ), lambda s: (0, s))
    return pl.pallas_call(
        attend_kernel,
        grid=(seqs,),
        in_specs=[col(QKV), col(HEAD_DIM), col(HEAD_DIM), pl.BlockSpec((1, 1, SEQ), lambda s: (s, 0, 0))],
        out_specs=[
            pl.BlockSpec((1, HEADS, ROWS, QB), lambda s: (s, 0, 0, 0)),
            col(D),
            col(D),
            col(KV_W),
            col(KV_W),
        ],
        out_shape=[
            jax.ShapeDtypeStruct((seqs, HEADS, ROWS, QB), BF16),
            jax.ShapeDtypeStruct((D, tokens), BF16),
            jax.ShapeDtypeStruct((D, tokens), BF16),
            jax.ShapeDtypeStruct((KV_W, tokens), BF16),
            jax.ShapeDtypeStruct((KV_W, tokens), BF16),
        ],
        scratch_shapes=[pltpu.VMEM((SEQ, SEQ), F32)],
        compiler_params=pltpu.CompilerParams(vmem_limit_bytes=40 * 2**20),
        cost_estimate=pl.CostEstimate(
            flops=seqs * 5_000_000_000, bytes_accessed=seqs * 8_000_000, transcendentals=seqs * 1_800_000
        ),
        name="attend_forward",
    )(qkv, cos, sin, start)


def attend_back_kernel(p_ref, o_ref, do_ref, q_ref, k_ref, v_ref, cos_ref, sin_ref, d_ref):
    cos, sin = cos_ref[...], sin_ref[...]

    def unturn(u):
        return (u * cos - turn_t(u) * sin).astype(BF16)

    for g in range(KV_HEADS):
        kt = k_ref[g * HEAD_DIM : (g + 1) * HEAD_DIM, :]
        v = v_ref[g * HEAD_DIM : (g + 1) * HEAD_DIM, :].T
        dk = [None, None]
        dv = [None, None]
        for j in range(GROUP):
            h = g * GROUP + j
            rows = slice(h * HEAD_DIM, (h + 1) * HEAD_DIM)
            dot_t = do_ref[rows, :]
            inner = jnp.sum(dot_t.astype(F32) * o_ref[rows, :].astype(F32), axis=0, keepdims=True)
            q = q_ref[rows, :].T
            do = dot_t.T
            dq = []
            for b, (q0, nk, r0) in enumerate(BLOCKS):
                share = p_ref[0, h, r0 : r0 + nk, :]
                dp = dot(v[:nk], dot_t[:, q0 : q0 + QB], 1, 0)
                ds = (share.astype(F32) * (dp - inner[:, q0 : q0 + QB])).astype(BF16)
                dq.append(dot(kt[:, :nk], ds, 1, 0))
                dk_new = dot(ds, q[q0 : q0 + QB], 1, 0)
                dv_new = dot(share, do[q0 : q0 + QB], 1, 0)
                dk[b] = dk_new if dk[b] is None else dk[b] + dk_new
                dv[b] = dv_new if dv[b] is None else dv[b] + dv_new
            d_ref[rows, :] = unturn(jnp.concatenate(dq, axis=1) * SCALE)
        dk_all = jnp.concatenate([dk[0] + dk[1][:QB], dk[1][QB:]], axis=0)
        dv_all = jnp.concatenate([dv[0] + dv[1][:QB], dv[1][QB:]], axis=0)
        d_ref[D + g * HEAD_DIM : D + (g + 1) * HEAD_DIM, :] = unturn(dk_all.T)
        d_ref[D + KV_W + g * HEAD_DIM : D + KV_W + (g + 1) * HEAD_DIM, :] = dv_all.T.astype(BF16)


def attend_backward(share, o, do, q, k, v, cos, sin):
    tokens = o.shape[1]
    seqs = tokens // SEQ
    col = lambda rows: pl.BlockSpec((rows, SEQ), lambda s: (0, s))
    return pl.pallas_call(
        attend_back_kernel,
        grid=(seqs,),
        in_specs=[
            pl.BlockSpec((1, HEADS, ROWS, QB), lambda s: (s, 0, 0, 0)),
            col(D),
            col(D),
            col(D),
            col(KV_W),
            col(KV_W),
            col(HEAD_DIM),
            col(HEAD_DIM),
        ],
        out_specs=col(QKV),
        out_shape=jax.ShapeDtypeStruct((QKV, tokens), BF16),
        compiler_params=pltpu.CompilerParams(vmem_limit_bytes=40 * 2**20),
        cost_estimate=pl.CostEstimate(
            flops=seqs * 10_000_000_000, bytes_accessed=seqs * 8_000_000, transcendentals=0
        ),
        name="attend_backward",
    )(share, o, do, q, k, v, cos, sin)


def swap(x, axis, size, bit):
    return lax.ppermute(x, axis, [(i, i ^ bit) for i in range(size)])


def bits_of(size):
    return [1 << n for n in range(size.bit_length() - 1)]


def gather_rows(block, size, order):
    me = lax.axis_index("dp")
    rows, width = block.shape
    held = block[None]
    lead = ()
    held = block
    for bit in order:
        other = swap(held, "dp", size, bit)
        upper = (me & bit) != 0
        held = jnp.stack([jnp.where(upper, other, held), jnp.where(upper, held, other)])
        lead = (bit,) + lead
    axes = sorted(range(len(lead)), key=lambda n: -lead[n])
    held = held.transpose(tuple(axes) + (len(lead), len(lead) + 1))
    return held.reshape(size * rows, width)


def scatter_rows(whole, size, rep, order):
    me = lax.axis_index("dp")
    rows, width = whole.shape[0] // size, whole.shape[1]
    bits = sorted(order, reverse=True)
    held = whole.astype(BF16).reshape((2,) * len(bits) + (rows, width))
    left = list(bits)
    for bit in order:
        at = left.index(bit)
        left.remove(bit)
        side = ((me & bit) != 0).astype(jnp.int32)
        keep = lax.dynamic_index_in_dim(held, side, at, keepdims=False)
        send = lax.dynamic_index_in_dim(held, 1 - side, at, keepdims=False)
        got = swap(send, "dp", size, bit)
        held = (keep.astype(F32) + got.astype(F32)).astype(BF16)
    got = swap(held, "rep", rep, 1)
    return held.astype(F32) + got.astype(F32)


def sum_small(x, size, rep):
    for bit in bits_of(size):
        x = x + swap(x, "dp", size, bit)
    return x + swap(x, "rep", rep, 1)


def per_device(
    size,
    rep,
    hidden_in,
    segment_ids,
    gain_attn,
    w_query,
    w_key,
    w_value,
    w_out,
    gain_mlp,
    w_gate,
    w_up,
    w_down,
    cotangent,
):
    by_rows = D % size == 0 and FF % size == 0 and size & (size - 1) == 0 and rep == 2
    if by_rows:
        bits = bits_of(size)
        down_order = bits[::-1]
        side_order = bits[:1:-1] + bits[1::-1] if len(bits) > 1 else bits
        part = D // size
        mats = [
            w.reshape(part, -1) for w in (w_query, w_key, w_value, w_out, w_gate, w_up)
        ]
        attn_w = gather_rows(jnp.concatenate(mats[:4], axis=1), size, down_order)
        mlp_w = gather_rows(jnp.concatenate(mats[4:], axis=1), size, side_order)
        down_w = gather_rows(w_down.reshape(FF // size, D), size, side_order)
    else:
        whole = [
            lax.all_gather(w, "dp", axis=0, tiled=True).reshape(D, -1)
            for w in (w_query, w_key, w_value, w_out, w_gate, w_up)
        ]
        attn_w = jnp.concatenate(whole[:4], axis=1)
        mlp_w = jnp.concatenate(whole[4:], axis=1)
        down_w = lax.all_gather(w_down, "dp", axis=0, tiled=True).reshape(FF, D)
    qkv_w, out_w = attn_w[:, :QKV], attn_w[:, QKV:]
    gate_w, up_w = mlp_w[:, :FF], mlp_w[:, FF:]

    seqs = hidden_in.shape[0]
    tokens = seqs * SEQ
    gain_first = gain_attn.astype(F32)
    gain_second = gain_mlp.astype(F32)

    start = jnp.sum(
        (segment_ids[:, None, :] < segment_ids[:, :, None]).astype(jnp.int32), axis=-1
    )
    place = (jnp.arange(SEQ, dtype=jnp.int32)[None, :] - start).astype(F32).reshape(1, tokens)
    inverse = THETA ** (-(jnp.arange(HALF, dtype=F32) * (2.0 / HEAD_DIM)))
    angle = inverse[:, None] * place
    cos, sin = jnp.cos(angle), jnp.sin(angle)
    cos = jnp.concatenate([cos, cos], axis=0)
    sin = jnp.concatenate([sin, sin], axis=0)

    x = hidden_in.reshape(tokens, D).astype(F32)
    r1 = lax.rsqrt(jnp.mean(x * x, axis=-1, keepdims=True) + EPS)
    h1 = (x * r1 * gain_first).astype(BF16)
    qkv = dot(qkv_w, h1, 0, 1)
    share, o, q, k, v = attend_forward(qkv, cos, sin, start.reshape(seqs, 1, SEQ))
    m = x + dot(o, out_w, 0, 0)
    r2 = lax.rsqrt(jnp.mean(m * m, axis=-1, keepdims=True) + EPS)
    h2 = (m * r2 * gain_second).astype(BF16)
    a = dot(h2, gate_w, 1, 0)
    b = dot(h2, up_w, 1, 0)
    s = jax.nn.sigmoid(a)
    c = (a * s * b).astype(BF16)
    result = (m + dot(c, down_w, 1, 0)).astype(BF16)

    gy = cotangent.reshape(tokens, D)
    d_down = dot(c, gy, 0, 0)
    dc = dot(gy, down_w, 1, 1)
    da = (dc * b * s * (1.0 + a * (1.0 - s))).astype(BF16)
    db = (dc * a * s).astype(BF16)
    d_gate = dot(h2, da, 0, 0)
    d_up = dot(h2, db, 0, 0)
    dh2 = dot(da, gate_w, 1, 1) + dot(db, up_w, 1, 1)
    g2 = jnp.sum(dh2 * m * r2, axis=0)
    e = dh2 * gain_second
    dm = gy.astype(F32) + r2 * (e - m * r2 * r2 * jnp.mean(e * m, axis=-1, keepdims=True))
    dmb = dm.astype(BF16)
    d_out = dot(o, dmb, 1, 0)
    do = dot(out_w, dmb, 1, 1).astype(BF16)
    dqkv = attend_backward(share, o, do, q, k, v, cos, sin)
    d_qkv = dot(h1, dqkv, 0, 1)
    dh1 = dot(dqkv, qkv_w, 0, 1)
    g1 = jnp.sum(dh1 * x * r1, axis=0)
    e1 = dh1 * gain_first
    dx = dm + r1 * (e1 - x * r1 * r1 * jnp.mean(e1 * x, axis=-1, keepdims=True))
    grad_hidden = dx.astype(BF16)

    if by_rows:
        up_order = bits
        d_down = scatter_rows(d_down, size, rep, up_order)
        d_gu = scatter_rows(
            jnp.concatenate([d_gate.astype(BF16), d_up.astype(BF16)], axis=1), size, rep, up_order
        )
        d_out = scatter_rows(d_out, size, rep, up_order)
        d_qkv = scatter_rows(d_qkv, size, rep, up_order)
        owned = [
            d_qkv[:, :D],
            d_qkv[:, D : D + KV_W],
            d_qkv[:, D + KV_W :],
            d_out,
            d_gu[:, :FF],
            d_gu[:, FF:],
            d_down,
        ]
        owned = [w.reshape(-1) for w in owned]
        gains = sum_small(jnp.stack([g1, g2]), size, rep)
    else:
        terms = [
            d_qkv[:, :D], d_qkv[:, D : D + KV_W], d_qkv[:, D + KV_W :], d_out, d_gate, d_up, d_down
        ]
        owned = []
        for term in terms:
            mine = lax.psum_scatter(term.reshape(-1), "dp", scatter_dimension=0, tiled=True)
            owned.append(lax.psum(mine.astype(BF16), "rep").astype(F32))
        gains = lax.psum(jnp.stack([g1, g2]), ("dp", "rep"))
    return (
        result.reshape(seqs, SEQ, D),
        grad_hidden.reshape(seqs, SEQ, D),
        gains[0],
        *owned[:4],
        gains[1],
        *owned[4:],
    )


def solution(mesh):
    flat = P("dp")
    seqs = P(("dp", "rep"), None, None)
    return jax.shard_map(
        functools.partial(per_device, mesh.shape["dp"], mesh.shape["rep"]),
        mesh=mesh,
        in_specs=(
            seqs,
            P(("dp", "rep"), None),
            P(),
            flat,
            flat,
            flat,
            flat,
            P(),
            flat,
            flat,
            flat,
            seqs,
        ),
        out_specs=(seqs, seqs, P(), flat, flat, flat, flat, P(), flat, flat, flat),
        check_vma=False,
    )
```

```python
import functools

import jax
import jax.numpy as jnp
from jax import lax
from jax.experimental import pallas as pl
from jax.experimental.pallas import tpu as pltpu
from jax.sharding import PartitionSpec as P

D = 576
HEADS = 9
KV_HEADS = 3
GROUP = HEADS // KV_HEADS
HEAD_DIM = 64
HALF = HEAD_DIM // 2
KV_W = KV_HEADS * HEAD_DIM
QKV = D + 2 * KV_W
FF = 1536
SEQ = 512
QB = 256

EPS = 1e-05
THETA = 100000.0
SCALE = HEAD_DIM ** (-0.5)
F32 = jnp.float32
BF16 = jnp.bfloat16

BLOCKS = ((0, QB, 0), (QB, SEQ, QB))
ROWS = QB + SEQ


def dot(a, b, ca, cb):
    return lax.dot_general(a, b, (((ca,), (cb,)), ((), ())), preferred_element_type=F32)


def turn_t(u):
    return jnp.concatenate([-u[HALF:], u[:HALF]], axis=0)


def attend_kernel(qkv_ref, cos_ref, sin_ref, start_ref, *refs):
    p_ref, o_ref, q_ref, k_ref, v_ref, bias_ref = refs[-6:]
    cos, sin = cos_ref[...], sin_ref[...]
    start = start_ref[0]
    key_at = lax.broadcasted_iota(jnp.int32, (SEQ, SEQ), 0)
    query_at = lax.broadcasted_iota(jnp.int32, (SEQ, SEQ), 1)
    ok = jnp.logical_and(key_at <= query_at, key_at >= start)
    bias_ref[...] = jnp.where(ok, 0.0, -1e30)
    v_ref[...] = qkv_ref[D + KV_W :, :].astype(BF16)
    for g in range(KV_HEADS):
        raw = qkv_ref[D + g * HEAD_DIM : D + (g + 1) * HEAD_DIM, :]
        kt = raw * cos + turn_t(raw) * sin
        k_ref[g * HEAD_DIM : (g + 1) * HEAD_DIM, :] = kt.astype(BF16)
        k = kt.T.astype(BF16)
        vt = v_ref[g * HEAD_DIM : (g + 1) * HEAD_DIM, :]
        for j in range(GROUP):
            h = g * GROUP + j
            rows = slice(h * HEAD_DIM, (h + 1) * HEAD_DIM)
            raw = qkv_ref[rows, :]
            qt = (raw * cos + turn_t(raw) * sin).astype(BF16) * jnp.asarray(SCALE, BF16)
            q_ref[rows, :] = qt
            for q0, nk, r0 in BLOCKS:
                st = dot(k[:nk], qt[:, q0 : q0 + QB], 1, 0) + bias_ref[:nk, q0 : q0 + QB]
                top = jnp.max(st, axis=0, keepdims=True)
                e = jnp.exp(st - top)
                total = jnp.sum(e, axis=0, keepdims=True)
                share = (e * (1.0 / total)).astype(BF16)
                p_ref[0, h, r0 : r0 + nk, :] = share
                o_ref[rows, q0 : q0 + QB] = dot(vt[:, :nk], share, 1, 0).astype(BF16)


def attend_forward(qkv, cos, sin, start, first, seqs, after, o_before):
    tokens = qkv.shape[1]
    col = lambda rows: pl.BlockSpec((rows, SEQ), lambda s: (0, s + first))
    own = lambda rows: pl.BlockSpec((rows, SEQ), lambda s: (0, s))
    extra = [*after] + ([] if o_before is None else [o_before])
    return pl.pallas_call(
        attend_kernel,
        grid=(seqs,),
        in_specs=[
            col(QKV),
            col(HEAD_DIM),
            col(HEAD_DIM),
            pl.BlockSpec((1, 1, SEQ), lambda s: (s + first, 0, 0)),
            *[pl.BlockSpec(memory_space=pl.ANY) for _ in extra],
        ],
        out_specs=[
            pl.BlockSpec((1, HEADS, ROWS, QB), lambda s: (s, 0, 0, 0)),
            col(D),
            own(D),
            own(KV_W),
            own(KV_W),
        ],
        out_shape=[
            jax.ShapeDtypeStruct((seqs, HEADS, ROWS, QB), BF16),
            jax.ShapeDtypeStruct((D, tokens), BF16),
            jax.ShapeDtypeStruct((D, seqs * SEQ), BF16),
            jax.ShapeDtypeStruct((KV_W, seqs * SEQ), BF16),
            jax.ShapeDtypeStruct((KV_W, seqs * SEQ), BF16),
        ],
        input_output_aliases={} if o_before is None else {3 + len(extra): 1},
        scratch_shapes=[pltpu.VMEM((SEQ, SEQ), F32)],
        compiler_params=pltpu.CompilerParams(vmem_limit_bytes=40 * 2**20),
        cost_estimate=pl.CostEstimate(
            flops=seqs * 5_000_000_000, bytes_accessed=seqs * 8_000_000, transcendentals=seqs * 1_800_000
        ),
        name="attend_forward",
    )(qkv, cos, sin, start, *extra)


def attend_back_kernel(p_ref, o_ref, do_ref, q_ref, k_ref, v_ref, cos_ref, sin_ref, *refs):
    d_ref = refs[-1]
    cos, sin = cos_ref[...], sin_ref[...]

    def unturn(u):
        return (u * cos - turn_t(u) * sin).astype(BF16)

    for g in range(KV_HEADS):
        kt = k_ref[g * HEAD_DIM : (g + 1) * HEAD_DIM, :]
        v = v_ref[g * HEAD_DIM : (g + 1) * HEAD_DIM, :].T
        dk = [None, None]
        dv = [None, None]
        for j in range(GROUP):
            h = g * GROUP + j
            rows = slice(h * HEAD_DIM, (h + 1) * HEAD_DIM)
            dot_t = do_ref[rows, :]
            inner = jnp.sum(dot_t.astype(F32) * o_ref[rows, :].astype(F32), axis=0, keepdims=True)
            q = q_ref[rows, :].T
            do = dot_t.T
            dq = []
            for b, (q0, nk, r0) in enumerate(BLOCKS):
                share = p_ref[0, h, r0 : r0 + nk, :]
                dp = dot(v[:nk], dot_t[:, q0 : q0 + QB], 1, 0)
                ds = (share.astype(F32) * (dp - inner[:, q0 : q0 + QB])).astype(BF16)
                dq.append(dot(kt[:, :nk], ds, 1, 0))
                dk_new = dot(ds, q[q0 : q0 + QB], 1, 0)
                dv_new = dot(share, do[q0 : q0 + QB], 1, 0)
                dk[b] = dk_new if dk[b] is None else dk[b] + dk_new
                dv[b] = dv_new if dv[b] is None else dv[b] + dv_new
            d_ref[rows, :] = unturn(jnp.concatenate(dq, axis=1) * SCALE)
        dk_all = jnp.concatenate([dk[0] + dk[1][:QB], dk[1][QB:]], axis=0)
        dv_all = jnp.concatenate([dv[0] + dv[1][:QB], dv[1][QB:]], axis=0)
        d_ref[D + g * HEAD_DIM : D + (g + 1) * HEAD_DIM, :] = unturn(dk_all.T)
        d_ref[D + KV_W + g * HEAD_DIM : D + KV_W + (g + 1) * HEAD_DIM, :] = dv_all.T.astype(BF16)


def attend_backward(share, o, do, q, k, v, cos, sin, first, after, d_before):
    tokens = o.shape[1]
    seqs = share.shape[0]
    col = lambda rows: pl.BlockSpec((rows, SEQ), lambda s: (0, s + first))
    own = lambda rows: pl.BlockSpec((rows, SEQ), lambda s: (0, s))
    extra = [*after] + ([] if d_before is None else [d_before])
    return pl.pallas_call(
        attend_back_kernel,
        grid=(seqs,),
        in_specs=[
            pl.BlockSpec((1, HEADS, ROWS, QB), lambda s: (s, 0, 0, 0)),
            col(D),
            col(D),
            own(D),
            own(KV_W),
            own(KV_W),
            col(HEAD_DIM),
            col(HEAD_DIM),
            *[pl.BlockSpec(memory_space=pl.ANY) for _ in extra],
        ],
        out_specs=col(QKV),
        out_shape=jax.ShapeDtypeStruct((QKV, tokens), BF16),
        input_output_aliases={} if d_before is None else {7 + len(extra): 0},
        compiler_params=pltpu.CompilerParams(vmem_limit_bytes=40 * 2**20),
        cost_estimate=pl.CostEstimate(
            flops=seqs * 10_000_000_000, bytes_accessed=seqs * 8_000_000, transcendentals=0
        ),
        name="attend_backward",
    )(share, o, do, q, k, v, cos, sin, *extra)


def swap(x, axis, size, bit):
    return lax.ppermute(x, axis, [(i, i ^ bit) for i in range(size)])


def bits_of(size):
    return [1 << n for n in range(size.bit_length() - 1)]


def upper(bit):
    return (lax.axis_index("dp") & bit) != 0


def gather_far(block, size):
    far = size // 4
    held = [block] + [swap(block, "dp", size, 4 * n) for n in range(1, far)]
    for bit in bits_of(far):
        up = upper(4 * bit)
        held = [jnp.where(up, held[n ^ bit], held[n]) for n in range(far)]
    return jnp.stack(held)


def gather_pair(held, size, bit):
    other = swap(held, "dp", size, bit)
    up = upper(bit)
    return jnp.stack([jnp.where(up, other, held), jnp.where(up, held, other)])


def gather_end(held):
    return held.transpose(2, 1, 0, 3, 4).reshape(-1, held.shape[-1])


def scatter_begin(whole, size):
    rows = whole.shape[0] // size
    return whole.astype(BF16).reshape(size // 4, 2, 2, rows, whole.shape[1])


def scatter_pair(held, size, bit, axis):
    side = upper(bit).astype(jnp.int32)
    keep = lax.dynamic_index_in_dim(held, side, axis, keepdims=False)
    send = lax.dynamic_index_in_dim(held, 1 - side, axis, keepdims=False)
    got = swap(send, "dp", size, bit)
    return (keep.astype(F32) + got.astype(F32)).astype(BF16)


def scatter_far(held, size):
    mine = lax.axis_index("dp") // 4
    block = lambda n: lax.dynamic_index_in_dim(held, mine ^ n, 0, keepdims=False)
    total = block(0).astype(F32)
    for n in range(1, size // 4):
        total = total + swap(block(n), "dp", size, 4 * n).astype(F32)
    return total.astype(BF16)


def scatter_rep(held, rep):
    return held.astype(F32) + swap(held, "rep", rep, 1).astype(F32)


def token(held):
    return held.reshape((-1,) + held.shape[-2:])[0, :16, :128]


def sum_small(x, size, rep):
    for bit in bits_of(size):
        x = x + swap(x, "dp", size, bit)
    return x + swap(x, "rep", rep, 1)


def per_device(
    size,
    rep,
    hidden_in,
    segment_ids,
    gain_attn,
    w_query,
    w_key,
    w_value,
    w_out,
    gain_mlp,
    w_gate,
    w_up,
    w_down,
    cotangent,
):
    by_rows = size >= 4 and D % size == 0 and FF % size == 0 and size & (size - 1) == 0 and rep == 2
    if by_rows:
        part = D // size
        mats = [
            w.reshape(part, -1) for w in (w_query, w_key, w_value, w_out, w_gate, w_up)
        ]
        attn_far = gather_far(jnp.concatenate(mats[:4], axis=1), size)
        mlp_block, attn_far = lax.optimization_barrier(
            (jnp.concatenate(mats[4:], axis=1), attn_far)
        )
        mlp_far = gather_far(mlp_block, size)
        attn_w = gather_end(gather_pair(gather_pair(attn_far, size, 2), size, 1))
        down_block, mlp_far = lax.optimization_barrier((w_down.reshape(FF // size, D), mlp_far))
        mlp_x = gather_pair(mlp_far, size, 2)
        down_far = gather_far(down_block, size)
        mlp_w = gather_end(gather_pair(mlp_x, size, 1))
        down_w = gather_end(gather_pair(gather_pair(down_far, size, 2), size, 1))
        after_first, after_second = (token(mlp_far),), (token(mlp_x), token(down_far))
    else:
        whole = [
            lax.all_gather(w, "dp", axis=0, tiled=True).reshape(D, -1)
            for w in (w_query, w_key, w_value, w_out, w_gate, w_up)
        ]
        attn_w = jnp.concatenate(whole[:4], axis=1)
        mlp_w = jnp.concatenate(whole[4:], axis=1)
        down_w = lax.all_gather(w_down, "dp", axis=0, tiled=True).reshape(FF, D)
        after_first, after_second = (), ()
    qkv_w, out_w = attn_w[:, :QKV], attn_w[:, QKV:]
    gate_w, up_w = mlp_w[:, :FF], mlp_w[:, FF:]

    seqs = hidden_in.shape[0]
    tokens = seqs * SEQ
    gain_first = gain_attn.astype(F32)
    gain_second = gain_mlp.astype(F32)

    start = jnp.sum(
        (segment_ids[:, None, :] < segment_ids[:, :, None]).astype(jnp.int32), axis=-1
    )
    place = (jnp.arange(SEQ, dtype=jnp.int32)[None, :] - start).astype(F32).reshape(1, tokens)
    inverse = THETA ** (-(jnp.arange(HALF, dtype=F32) * (2.0 / HEAD_DIM)))
    angle = inverse[:, None] * place
    cos, sin = jnp.cos(angle), jnp.sin(angle)
    cos = jnp.concatenate([cos, cos], axis=0)
    sin = jnp.concatenate([sin, sin], axis=0)

    x = hidden_in.reshape(tokens, D).astype(F32)
    r1 = lax.rsqrt(jnp.mean(x * x, axis=-1, keepdims=True) + EPS)
    h1 = (x * r1 * gain_first).astype(BF16)
    qkv = dot(qkv_w, h1, 0, 1)
    start = start.reshape(seqs, 1, SEQ)
    half = seqs // 2
    share0, o, q0, k0, v0 = attend_forward(qkv, cos, sin, start, 0, half, after_first, None)
    share1, o, q1, k1, v1 = attend_forward(
        qkv, cos, sin, start, half, seqs - half, after_second, o
    )
    m = x + dot(o, out_w, 0, 0)
    r2 = lax.rsqrt(jnp.mean(m * m, axis=-1, keepdims=True) + EPS)
    h2 = (m * r2 * gain_second).astype(BF16)
    a = dot(h2, gate_w, 1, 0)
    b = dot(h2, up_w, 1, 0)
    s = jax.nn.sigmoid(a)
    c = (a * s * b).astype(BF16)
    result = (m + dot(c, down_w, 1, 0)).astype(BF16)

    gy = cotangent.reshape(tokens, D)
    d_down = dot(c, gy, 0, 0)
    if by_rows:
        d_down, gy = lax.optimization_barrier((d_down.astype(BF16), gy))
        down_core = scatter_pair(scatter_begin(d_down, size), size, 1, 2)
    dc = dot(gy, down_w, 1, 1)
    da = (dc * b * s * (1.0 + a * (1.0 - s))).astype(BF16)
    db = (dc * a * s).astype(BF16)
    d_gate = dot(h2, da, 0, 0)
    d_up = dot(h2, db, 0, 0)
    after_first, after_second = (), ()
    if by_rows:
        d_gu = jnp.concatenate([d_gate.astype(BF16), d_up.astype(BF16)], axis=1)
        d_gu, down_core, da, db = lax.optimization_barrier((d_gu, down_core, da, db))
        gu_core = scatter_pair(scatter_begin(d_gu, size), size, 1, 2)
        down_x = scatter_pair(down_core, size, 2, 1)
    dh2 = dot(da, gate_w, 1, 1) + dot(db, up_w, 1, 1)
    g2 = jnp.sum(dh2 * m * r2, axis=0)
    e = dh2 * gain_second
    dm = gy.astype(F32) + r2 * (e - m * r2 * r2 * jnp.mean(e * m, axis=-1, keepdims=True))
    dmb = dm.astype(BF16)
    d_out = dot(o, dmb, 1, 0)
    do = dot(out_w, dmb, 1, 1).astype(BF16)
    if by_rows:
        gu_x = scatter_pair(gu_core, size, 2, 1)
        down_z = scatter_far(down_x, size)
        out_core = scatter_pair(scatter_begin(d_out, size), size, 1, 2)
        after_first = (token(gu_core), token(down_x))
        after_second = (token(gu_x), token(out_core), token(down_z))
    dqkv = attend_backward(share0, o, do, q0, k0, v0, cos, sin, 0, after_first, None)
    dqkv = attend_backward(share1, o, do, q1, k1, v1, cos, sin, half, after_second, dqkv)
    d_qkv = dot(h1, dqkv, 0, 1)
    dh1 = dot(dqkv, qkv_w, 0, 1)
    g1 = jnp.sum(dh1 * x * r1, axis=0)
    e1 = dh1 * gain_first
    dx = dm + r1 * (e1 - x * r1 * r1 * jnp.mean(e1 * x, axis=-1, keepdims=True))
    grad_hidden = dx.astype(BF16)

    if by_rows:
        d_down = scatter_rep(down_z, rep)
        d_gu = scatter_rep(scatter_far(gu_x, size), rep)
        d_out = scatter_rep(scatter_far(scatter_pair(out_core, size, 2, 1), size), rep)
        d_qkv = scatter_pair(scatter_begin(d_qkv, size), size, 1, 2)
        d_qkv = scatter_rep(scatter_far(scatter_pair(d_qkv, size, 2, 1), size), rep)
        owned = [
            d_qkv[:, :D],
            d_qkv[:, D : D + KV_W],
            d_qkv[:, D + KV_W :],
            d_out,
            d_gu[:, :FF],
            d_gu[:, FF:],
            d_down,
        ]
        owned = [w.reshape(-1) for w in owned]
        gains = sum_small(jnp.stack([g1, g2]), size, rep)
    else:
        terms = [
            d_qkv[:, :D], d_qkv[:, D : D + KV_W], d_qkv[:, D + KV_W :], d_out, d_gate, d_up, d_down
        ]
        owned = []
        for term in terms:
            mine = lax.psum_scatter(term.reshape(-1), "dp", scatter_dimension=0, tiled=True)
            owned.append(lax.psum(mine.astype(BF16), "rep").astype(F32))
        gains = lax.psum(jnp.stack([g1, g2]), ("dp", "rep"))
    return (
        result.reshape(seqs, SEQ, D),
        grad_hidden.reshape(seqs, SEQ, D),
        gains[0],
        *owned[:4],
        gains[1],
        *owned[4:],
    )


def solution(mesh):
    flat = P("dp")
    seqs = P(("dp", "rep"), None, None)
    return jax.shard_map(
        functools.partial(per_device, mesh.shape["dp"], mesh.shape["rep"]),
        mesh=mesh,
        in_specs=(
            seqs,
            P(("dp", "rep"), None),
            P(),
            flat,
            flat,
            flat,
            flat,
            P(),
            flat,
            flat,
            flat,
            seqs,
        ),
        out_specs=(seqs, seqs, P(), flat, flat, flat, flat, P(), flat, flat, flat),
        check_vma=False,
    )
```

```python
import functools

import jax
import jax.numpy as jnp
from jax import lax
from jax.experimental import pallas as pl
from jax.experimental.pallas import tpu as pltpu
from jax.sharding import PartitionSpec as P

D = 576
HEADS = 9
KV_HEADS = 3
GROUP = HEADS // KV_HEADS
HEAD_DIM = 64
HALF = HEAD_DIM // 2
KV_W = KV_HEADS * HEAD_DIM
QKV = D + 2 * KV_W
FF = 1536
SEQ = 512
QB = 256

EPS = 1e-05
THETA = 100000.0
SCALE = HEAD_DIM ** (-0.5)
F32 = jnp.float32
BF16 = jnp.bfloat16

BLOCKS = ((0, QB, 0), (QB, SEQ, QB))
ROWS = QB + SEQ


def dot(a, b, ca, cb):
    return lax.dot_general(a, b, (((ca,), (cb,)), ((), ())), preferred_element_type=F32)


def turn_t(u):
    return jnp.concatenate([-u[HALF:], u[:HALF]], axis=0)


def attend_kernel(qkv_ref, cos_ref, sin_ref, start_ref, *refs):
    p_ref, o_ref, q_ref, k_ref, v_ref, bias_ref = refs[-6:]
    cos, sin = cos_ref[...], sin_ref[...]
    start = start_ref[0]
    key_at = lax.broadcasted_iota(jnp.int32, (SEQ, SEQ), 0)
    query_at = lax.broadcasted_iota(jnp.int32, (SEQ, SEQ), 1)
    ok = jnp.logical_and(key_at <= query_at, key_at >= start)
    bias_ref[...] = jnp.where(ok, 0.0, -1e30)
    v_ref[...] = qkv_ref[D + KV_W :, :].astype(BF16)
    for g in range(KV_HEADS):
        raw = qkv_ref[D + g * HEAD_DIM : D + (g + 1) * HEAD_DIM, :]
        kt = raw * cos + turn_t(raw) * sin
        k_ref[g * HEAD_DIM : (g + 1) * HEAD_DIM, :] = kt.astype(BF16)
        k = kt.T.astype(BF16)
        vt = v_ref[g * HEAD_DIM : (g + 1) * HEAD_DIM, :]
        for j in range(GROUP):
            h = g * GROUP + j
            rows = slice(h * HEAD_DIM, (h + 1) * HEAD_DIM)
            raw = qkv_ref[rows, :]
            qt = (raw * cos + turn_t(raw) * sin).astype(BF16) * jnp.asarray(SCALE, BF16)
            q_ref[rows, :] = qt
            for q0, nk, r0 in BLOCKS:
                st = dot(k[:nk], qt[:, q0 : q0 + QB], 1, 0) + bias_ref[:nk, q0 : q0 + QB]
                top = jnp.max(st, axis=0, keepdims=True)
                e = jnp.exp(st - top)
                total = jnp.sum(e, axis=0, keepdims=True)
                share = (e * (1.0 / total)).astype(BF16)
                p_ref[0, h, r0 : r0 + nk, :] = share
                o_ref[rows, q0 : q0 + QB] = dot(vt[:, :nk], share, 1, 0).astype(BF16)


def attend_forward(qkv, cos, sin, start, first, seqs, after, o_before):
    tokens = qkv.shape[1]
    col = lambda rows: pl.BlockSpec((rows, SEQ), lambda s: (0, s + first))
    own = lambda rows: pl.BlockSpec((rows, SEQ), lambda s: (0, s))
    extra = [*after] + ([] if o_before is None else [o_before])
    return pl.pallas_call(
        attend_kernel,
        grid=(seqs,),
        in_specs=[
            col(QKV),
            col(HEAD_DIM),
            col(HEAD_DIM),
            pl.BlockSpec((1, 1, SEQ), lambda s: (s + first, 0, 0)),
            *[pl.BlockSpec(memory_space=pl.ANY) for _ in extra],
        ],
        out_specs=[
            pl.BlockSpec((1, HEADS, ROWS, QB), lambda s: (s, 0, 0, 0)),
            col(D),
            own(D),
            own(KV_W),
            own(KV_W),
        ],
        out_shape=[
            jax.ShapeDtypeStruct((seqs, HEADS, ROWS, QB), BF16),
            jax.ShapeDtypeStruct((D, tokens), BF16),
            jax.ShapeDtypeStruct((D, seqs * SEQ), BF16),
            jax.ShapeDtypeStruct((KV_W, seqs * SEQ), BF16),
            jax.ShapeDtypeStruct((KV_W, seqs * SEQ), BF16),
        ],
        input_output_aliases={} if o_before is None else {3 + len(extra): 1},
        scratch_shapes=[pltpu.VMEM((SEQ, SEQ), F32)],
        compiler_params=pltpu.CompilerParams(vmem_limit_bytes=40 * 2**20),
        cost_estimate=pl.CostEstimate(
            flops=seqs * 5_000_000_000, bytes_accessed=seqs * 8_000_000, transcendentals=seqs * 1_800_000
        ),
        name="attend_forward",
    )(qkv, cos, sin, start, *extra)


def attend_back_kernel(p_ref, o_ref, do_ref, q_ref, k_ref, v_ref, cos_ref, sin_ref, *refs):
    d_ref = refs[-1]
    cos, sin = cos_ref[...], sin_ref[...]

    def unturn(u):
        return (u * cos - turn_t(u) * sin).astype(BF16)

    for g in range(KV_HEADS):
        kt = k_ref[g * HEAD_DIM : (g + 1) * HEAD_DIM, :]
        v = v_ref[g * HEAD_DIM : (g + 1) * HEAD_DIM, :].T
        dk = [None, None]
        dv = [None, None]
        for j in range(GROUP):
            h = g * GROUP + j
            rows = slice(h * HEAD_DIM, (h + 1) * HEAD_DIM)
            dot_t = do_ref[rows, :]
            inner = jnp.sum(dot_t.astype(F32) * o_ref[rows, :].astype(F32), axis=0, keepdims=True)
            q = q_ref[rows, :].T
            do = dot_t.T
            dq = []
            for b, (q0, nk, r0) in enumerate(BLOCKS):
                share = p_ref[0, h, r0 : r0 + nk, :]
                dp = dot(v[:nk], dot_t[:, q0 : q0 + QB], 1, 0)
                ds = (share.astype(F32) * (dp - inner[:, q0 : q0 + QB])).astype(BF16)
                dq.append(dot(kt[:, :nk], ds, 1, 0))
                dk_new = dot(ds, q[q0 : q0 + QB], 1, 0)
                dv_new = dot(share, do[q0 : q0 + QB], 1, 0)
                dk[b] = dk_new if dk[b] is None else dk[b] + dk_new
                dv[b] = dv_new if dv[b] is None else dv[b] + dv_new
            d_ref[rows, :] = unturn(jnp.concatenate(dq, axis=1) * SCALE)
        dk_all = jnp.concatenate([dk[0] + dk[1][:QB], dk[1][QB:]], axis=0)
        dv_all = jnp.concatenate([dv[0] + dv[1][:QB], dv[1][QB:]], axis=0)
        d_ref[D + g * HEAD_DIM : D + (g + 1) * HEAD_DIM, :] = unturn(dk_all.T)
        d_ref[D + KV_W + g * HEAD_DIM : D + KV_W + (g + 1) * HEAD_DIM, :] = dv_all.T.astype(BF16)


def attend_backward(share, o, do, q, k, v, cos, sin, first, after, d_before):
    tokens = o.shape[1]
    seqs = share.shape[0]
    col = lambda rows: pl.BlockSpec((rows, SEQ), lambda s: (0, s + first))
    own = lambda rows: pl.BlockSpec((rows, SEQ), lambda s: (0, s))
    extra = [*after] + ([] if d_before is None else [d_before])
    return pl.pallas_call(
        attend_back_kernel,
        grid=(seqs,),
        in_specs=[
            pl.BlockSpec((1, HEADS, ROWS, QB), lambda s: (s, 0, 0, 0)),
            col(D),
            col(D),
            own(D),
            own(KV_W),
            own(KV_W),
            col(HEAD_DIM),
            col(HEAD_DIM),
            *[pl.BlockSpec(memory_space=pl.ANY) for _ in extra],
        ],
        out_specs=col(QKV),
        out_shape=jax.ShapeDtypeStruct((QKV, tokens), BF16),
        input_output_aliases={} if d_before is None else {7 + len(extra): 0},
        compiler_params=pltpu.CompilerParams(vmem_limit_bytes=40 * 2**20),
        cost_estimate=pl.CostEstimate(
            flops=seqs * 10_000_000_000, bytes_accessed=seqs * 8_000_000, transcendentals=0
        ),
        name="attend_backward",
    )(share, o, do, q, k, v, cos, sin, *extra)


def swap(x, axis, size, bit):
    return lax.ppermute(x, axis, [(i, i ^ bit) for i in range(size)])


def bits_of(size):
    return [1 << n for n in range(size.bit_length() - 1)]


def upper(bit):
    return (lax.axis_index("dp") & bit) != 0


def gather_far(block, size):
    far = size // 4
    held = [block] + [swap(block, "dp", size, 4 * n) for n in range(1, far)]
    for bit in bits_of(far):
        up = upper(4 * bit)
        held = [jnp.where(up, held[n ^ bit], held[n]) for n in range(far)]
    return jnp.stack(held)


def gather_pair(held, size, bit):
    other = swap(held, "dp", size, bit)
    up = upper(bit)
    return jnp.stack([jnp.where(up, other, held), jnp.where(up, held, other)])


def gather_end(held):
    return held.transpose(2, 1, 0, 3, 4).reshape(-1, held.shape[-1])


def scatter_begin(whole, size):
    rows = whole.shape[0] // size
    return whole.astype(BF16).reshape(size // 4, 2, 2, rows, whole.shape[1])


def scatter_pair(held, size, bit, axis):
    side = upper(bit).astype(jnp.int32)
    keep = lax.dynamic_index_in_dim(held, side, axis, keepdims=False)
    send = lax.dynamic_index_in_dim(held, 1 - side, axis, keepdims=False)
    got = swap(send, "dp", size, bit)
    return (keep.astype(F32) + got.astype(F32)).astype(BF16)


def scatter_far(held, size):
    mine = lax.axis_index("dp") // 4
    block = lambda n: lax.dynamic_index_in_dim(held, mine ^ n, 0, keepdims=False)
    total = block(0).astype(F32)
    for n in range(1, size // 4):
        total = total + swap(block(n), "dp", size, 4 * n).astype(F32)
    return total.astype(BF16)


def scatter_rep(held, rep):
    return held.astype(F32) + swap(held, "rep", rep, 1).astype(F32)


def token(held):
    return held.reshape((-1,) + held.shape[-2:])[0, :16, :128]


def sum_small(x, size, rep):
    for bit in bits_of(size):
        x = x + swap(x, "dp", size, bit)
    return x + swap(x, "rep", rep, 1)


def per_device(
    size,
    rep,
    hidden_in,
    segment_ids,
    gain_attn,
    w_query,
    w_key,
    w_value,
    w_out,
    gain_mlp,
    w_gate,
    w_up,
    w_down,
    cotangent,
):
    by_rows = size >= 4 and D % size == 0 and FF % size == 0 and size & (size - 1) == 0 and rep == 2
    if by_rows:
        part = D // size
        mats = [
            w.reshape(part, -1) for w in (w_query, w_key, w_value, w_out, w_gate, w_up)
        ]
        attn_far = gather_far(jnp.concatenate(mats[:4], axis=1), size)
        attn_w = gather_end(gather_pair(gather_pair(attn_far, size, 2), size, 1))
        mlp_block, down_block, attn_w = lax.optimization_barrier(
            (jnp.concatenate(mats[4:], axis=1), w_down.reshape(FF // size, D), attn_w)
        )
        mlp_far = gather_far(mlp_block, size)
    else:
        whole = [
            lax.all_gather(w, "dp", axis=0, tiled=True).reshape(D, -1)
            for w in (w_query, w_key, w_value, w_out, w_gate, w_up)
        ]
        attn_w = jnp.concatenate(whole[:4], axis=1)
        gate_w, up_w = whole[4:]
        down_w = lax.all_gather(w_down, "dp", axis=0, tiled=True).reshape(FF, D)
    qkv_w, out_w = attn_w[:, :QKV], attn_w[:, QKV:]

    seqs = hidden_in.shape[0]
    tokens = seqs * SEQ
    gain_first = gain_attn.astype(F32)
    gain_second = gain_mlp.astype(F32)

    start = jnp.sum(
        (segment_ids[:, None, :] < segment_ids[:, :, None]).astype(jnp.int32), axis=-1
    )
    place = (jnp.arange(SEQ, dtype=jnp.int32)[None, :] - start).astype(F32).reshape(1, tokens)
    inverse = THETA ** (-(jnp.arange(HALF, dtype=F32) * (2.0 / HEAD_DIM)))
    angle = inverse[:, None] * place
    cos, sin = jnp.cos(angle), jnp.sin(angle)
    cos = jnp.concatenate([cos, cos], axis=0)
    sin = jnp.concatenate([sin, sin], axis=0)

    x = hidden_in.reshape(tokens, D).astype(F32)
    r1 = lax.rsqrt(jnp.mean(x * x, axis=-1, keepdims=True) + EPS)
    h1 = (x * r1 * gain_first).astype(BF16)
    qkv = dot(qkv_w, h1, 0, 1)
    start = start.reshape(seqs, 1, SEQ)
    half = seqs // 2
    share0, o, q0, k0, v0 = attend_forward(qkv, cos, sin, start, 0, half, (), None)
    if by_rows:
        mlp_far, down_block, o = lax.optimization_barrier((mlp_far, down_block, o))
        mlp_x = gather_pair(mlp_far, size, 2)
        down_far = gather_far(down_block, size)
    share1, o, q1, k1, v1 = attend_forward(
        qkv, cos, sin, start, half, seqs - half, (), o
    )
    if by_rows:
        mlp_x, down_far, o = lax.optimization_barrier((mlp_x, down_far, o))
        mlp_w = gather_end(gather_pair(mlp_x, size, 1))
        gate_w, up_w = mlp_w[:, :FF], mlp_w[:, FF:]
        down_w = gather_end(gather_pair(gather_pair(down_far, size, 2), size, 1))
    m = x + dot(o, out_w, 0, 0)
    r2 = lax.rsqrt(jnp.mean(m * m, axis=-1, keepdims=True) + EPS)
    h2 = (m * r2 * gain_second).astype(BF16)
    a = dot(h2, gate_w, 1, 0)
    b = dot(h2, up_w, 1, 0)
    s = jax.nn.sigmoid(a)
    c = (a * s * b).astype(BF16)
    result = (m + dot(c, down_w, 1, 0)).astype(BF16)

    gy = cotangent.reshape(tokens, D)
    d_down = dot(c, gy, 0, 0)
    dc = dot(gy, down_w, 1, 1)
    da = (dc * b * s * (1.0 + a * (1.0 - s))).astype(BF16)
    db = (dc * a * s).astype(BF16)
    d_gate = dot(h2, da, 0, 0)
    d_up = dot(h2, db, 0, 0)
    dh2 = dot(da, gate_w, 1, 1) + dot(db, up_w, 1, 1)
    g2 = jnp.sum(dh2 * m * r2, axis=0)
    e = dh2 * gain_second
    dm = gy.astype(F32) + r2 * (e - m * r2 * r2 * jnp.mean(e * m, axis=-1, keepdims=True))
    dmb = dm.astype(BF16)
    d_out = dot(o, dmb, 1, 0)
    do = dot(out_w, dmb, 1, 1).astype(BF16)
    after_first, after_second = (), ()
    if by_rows:
        d_gu = jnp.concatenate([d_gate.astype(BF16), d_up.astype(BF16)], axis=1)
        d_down, d_gu, d_out, do = lax.optimization_barrier(
            (d_down.astype(BF16), d_gu, d_out.astype(BF16), do)
        )
        down_core = scatter_pair(scatter_begin(d_down, size), size, 1, 2)
        gu_core = scatter_pair(scatter_begin(d_gu, size), size, 1, 2)
        after_first = (token(gu_core), token(down_core))
    dqkv = attend_backward(share0, o, do, q0, k0, v0, cos, sin, 0, after_first, None)
    if by_rows:
        down_x = scatter_pair(down_core, size, 2, 1)
        gu_x = scatter_pair(gu_core, size, 2, 1)
        d_out, down_x, dqkv = lax.optimization_barrier((d_out, down_x, dqkv))
        out_core = scatter_pair(scatter_begin(d_out, size), size, 1, 2)
    dqkv = attend_backward(share1, o, do, q1, k1, v1, cos, sin, half, after_second, dqkv)
    if by_rows:
        gu_x, out_core, dqkv = lax.optimization_barrier((gu_x, out_core, dqkv))
        down_z = scatter_far(down_x, size)
    d_qkv = dot(h1, dqkv, 0, 1)
    dh1 = dot(dqkv, qkv_w, 0, 1)
    g1 = jnp.sum(dh1 * x * r1, axis=0)
    e1 = dh1 * gain_first
    dx = dm + r1 * (e1 - x * r1 * r1 * jnp.mean(e1 * x, axis=-1, keepdims=True))
    grad_hidden = dx.astype(BF16)

    if by_rows:
        d_down = scatter_rep(down_z, rep)
        d_gu = scatter_rep(scatter_far(gu_x, size), rep)
        d_out = scatter_rep(scatter_far(scatter_pair(out_core, size, 2, 1), size), rep)
        d_qkv = scatter_pair(scatter_begin(d_qkv, size), size, 1, 2)
        d_qkv = scatter_rep(scatter_far(scatter_pair(d_qkv, size, 2, 1), size), rep)
        owned = [
            d_qkv[:, :D],
            d_qkv[:, D : D + KV_W],
            d_qkv[:, D + KV_W :],
            d_out,
            d_gu[:, :FF],
            d_gu[:, FF:],
            d_down,
        ]
        owned = [w.reshape(-1) for w in owned]
        gains = sum_small(jnp.stack([g1, g2]), size, rep)
    else:
        terms = [
            d_qkv[:, :D], d_qkv[:, D : D + KV_W], d_qkv[:, D + KV_W :], d_out, d_gate, d_up, d_down
        ]
        owned = []
        for term in terms:
            mine = lax.psum_scatter(term.reshape(-1), "dp", scatter_dimension=0, tiled=True)
            owned.append(lax.psum(mine.astype(BF16), "rep").astype(F32))
        gains = lax.psum(jnp.stack([g1, g2]), ("dp", "rep"))
    return (
        result.reshape(seqs, SEQ, D),
        grad_hidden.reshape(seqs, SEQ, D),
        gains[0],
        *owned[:4],
        gains[1],
        *owned[4:],
    )


def solution(mesh):
    flat = P("dp")
    seqs = P(("dp", "rep"), None, None)
    return jax.shard_map(
        functools.partial(per_device, mesh.shape["dp"], mesh.shape["rep"]),
        mesh=mesh,
        in_specs=(
            seqs,
            P(("dp", "rep"), None),
            P(),
            flat,
            flat,
            flat,
            flat,
            P(),
            flat,
            flat,
            flat,
            seqs,
        ),
        out_specs=(seqs, seqs, P(), flat, flat, flat, flat, P(), flat, flat, flat),
        check_vma=False,
    )
```
